256 devices in a mesh: pipe: 4 (over y_hi, core), expert: 64 (over z, x, y_lo).
Axes of the slice: x: 4, y: 4 (y_hi: 2, y_lo: 2; y = y_hi * 2 + y_lo), z: 8, core: 2. Of those that a mesh axis runs over, the one named last changes fastest.
Arguments:
- act_a: bfloat16 [4, 4096, 3584], P('pipe', 'expert'), may hold values from -6 to 6
- ids_a: int32 [4, 4096, 2], P('pipe', 'expert'), may hold values from 0 to 15, all different within a row; in each aligned block of 64 rows (0 to 63, 64 to 127, ..., all dimensions but the last counted through in order) at most 10 rows name the same one
- act_b: bfloat16 [4, 4096, 3584], P('pipe', 'expert'), may hold values from -6 to 6
- cot_b: bfloat16 [4, 4096, 3584], P('pipe', 'expert'), may hold values from -6 to 6
- ids_b: int32 [4, 4096, 2], P('pipe', 'expert'), may hold values from 0 to 15, all different within a row; in each aligned block of 64 rows (0 to 63, 64 to 127, ..., all dimensions but the last counted through in order) at most 10 rows name the same one
- norm_gain: bfloat16 [4, 3584], P('pipe'), may hold values from 0.5 to 1.5
- router: bfloat16 [4, 3584, 16], P('pipe'), may hold values from -0.09375 to 0.09375
- w_gate: bfloat16 [4, 64, 3584, 256], P('pipe', 'expert'), may hold values from -0.09375 to 0.09375
- w_up: bfloat16 [4, 64, 3584, 256], P('pipe', 'expert'), may hold values from -0.09375 to 0.09375
- w_down: bfloat16 [4, 64, 256, 3584], P('pipe', 'expert'), may hold values from -0.1875 to 0.1875
Outputs:
- next_a: bfloat16 [4, 4096, 3584], P('pipe', 'expert')
- next_b: bfloat16 [4, 4096, 3584], P('pipe', 'expert')
The draws below stay inside these ranges and needn't reach their ends.
Inputs may be any that keep to these rules, and one draw needn't show every extreme that they name: `ids_a`: each row names 2 different experts. Within the 64 rows of one device (aligned blocks along the relay and token dimensions taken together) no expert is named by more than 10 rows, a bound that some block reaches of them. `ids_b`: as for ids_a.
All inputs are finite; a program needn't handle non-finite values.
Results may differ from the reference program's by a relative error of at most 0.013.
Values may be sent and summed in bfloat16 or wider, within the bound.
No kernel may reach another device: no remote copies, remote signals or barrier semaphores. Data moves between devices by JAX's collectives and lax.ppermute only.
A program may use at most 128 MiB of HBM per device.

```python
import math
import jax
import jax.numpy as jnp
import numpy as np
from jax import lax

D = 3584
FF = 1024
SPLIT = 4
TOP = 2
TOK_DEV = 64
FF_DEV = 256
EXPERTS = 16
TOKENS = 4096
CAP = 10
N_PIPE = 4
N_EXPERT = 64


def shard_levels(rng, dims, split, smallest, largest):
    def one(position, blocks):
        draws = jax.random.uniform(jax.random.fold_in(jax.random.fold_in(rng, 6), position), (blocks,), jnp.float32, smallest / len(split), largest / len(split))
        return jnp.repeat(jnp.exp(draws), dims[position] // blocks).reshape((-1,) + (1,) * (len(dims) - position - 1))

    level = one(*split[0])
    for cut in split[1:]:
        level = level * one(*cut)
    return level


def deal_out(stream_key, own, number, rows, amount, top, bound, skew):
    order = jax.random.permutation(stream_key, amount)
    heavy_load, common = portions_of(amount, rows * top, bound, skew, True), portions_of(amount, rows * top, bound, skew, False)
    places = jnp.arange(amount)

    def named(sizes, rotation):
        used = int((sizes > 0).sum())
        fixed = max(1, used // 4)
        passed = fixed + (places - fixed + rotation * (used - fixed)) % max(1, amount - fixed)
        return jnp.zeros((amount,), jnp.int32).at[order[jnp.where(places < fixed, places, passed)]].set(jnp.asarray(sizes, jnp.int32))

    sizes = jnp.where(number % 4 == 0, named(heavy_load, number // 4), named(common, number - number // 4 - 1))
    mixed = jax.random.permutation(jax.random.fold_in(own, 3), amount)
    source_of, taker = mixed[0:amount // 2 * 2:2], mixed[1:amount // 2 * 2:2]
    room = jnp.minimum(sizes[source_of] - 1, bound - sizes[taker]) // 2
    room = jnp.where((source_of == order[0]) | (taker == order[0]) | (sizes[taker] == 0), 0, jnp.maximum(room, 0))
    passed = jax.random.randint(jax.random.fold_in(own, 4), (amount // 2,), 0, 1 << 20) % (room + 1)
    sizes = sizes.at[source_of].add(-passed).at[taker].add(passed)
    members = jnp.searchsorted(jnp.cumsum(sizes), jnp.arange(rows * top), side="right").astype(jnp.int32)
    grid = members.reshape(top, rows).T
    grid = grid[jax.random.permutation(jax.random.fold_in(own, 1), rows)]
    rotation = jax.random.randint(jax.random.fold_in(own, 2), (rows, 1), 0, top)
    return jnp.take_along_axis(grid, (jnp.arange(top)[None, :] + rotation) % top, axis=1)


def portions_of(number_of, total, bound, lean, full):
    loads = [(1 << 20) // math.isqrt(standing ** lean) + 1 for standing in range(1, number_of + 1)]
    largest = bound if full else min(bound, max(-(-total // number_of), total * loads[0] // sum(loads)))
    least = 1 if total - largest >= number_of - 1 else 0
    counts, rest = [largest] + [least] * (number_of - 1), total - largest - least * (number_of - 1)
    while rest > 0:
        free = [i for i in range(1, number_of) if counts[i] < largest] or [i for i in range(1, number_of) if counts[i] < bound]
        whole, remaining = sum([loads[i] for i in free]), rest
        for i in free:
            addition = min(bound - counts[i], max(1, remaining * loads[i] // whole), rest)
            counts[i] = counts[i] + addition
            rest = rest - addition
    return np.array(counts)


def gaussian(key, dims, deviation, limit, split=(), kind=jnp.bfloat16):
    result = jax.random.normal(key, dims, jnp.float32) * deviation
    if len(split) > 0:
        result = shard_levels(key, dims, split, -0.22, 0.18) * result
    return jnp.clip(result, min=-limit, max=limit).astype(kind)


def setup_inputs(seed: int = 0) -> dict:
    streams_of = jax.random.split(jax.random.key(seed), 11)
    act_a = gaussian(streams_of[0], (N_PIPE, TOKENS, D), 1.0, 6.0, ((0, 4), (1, 64)))
    ids_a_keys = jax.random.split(jax.random.fold_in(streams_of[1], 1), N_PIPE * TOKENS // TOK_DEV)
    ids_a_turns = jax.random.permutation(jax.random.fold_in(streams_of[1], 3), N_PIPE * TOKENS // TOK_DEV)
    ids_a = jax.vmap(lambda own, number: deal_out(jax.random.fold_in(streams_of[1], 2), own, number, TOK_DEV, EXPERTS, TOP, CAP, 2))(ids_a_keys, ids_a_turns).reshape((N_PIPE, TOKENS, TOP))
    act_b = gaussian(streams_of[2], (N_PIPE, TOKENS, D), 1.0, 6.0, ((0, 4), (1, 64)))
    cot_b = gaussian(streams_of[3], (N_PIPE, TOKENS, D), 1.0, 6.0, ((0, 4), (1, 64)))
    ids_b_keys = jax.random.split(jax.random.fold_in(streams_of[4], 1), N_PIPE * TOKENS // TOK_DEV)
    ids_b_turns = jax.random.permutation(jax.random.fold_in(streams_of[4], 3), N_PIPE * TOKENS // TOK_DEV)
    ids_b = jax.vmap(lambda own, number: deal_out(jax.random.fold_in(streams_of[4], 2), own, number, TOK_DEV, EXPERTS, TOP, CAP, 2))(ids_b_keys, ids_b_turns).reshape((N_PIPE, TOKENS, TOP))
    norm_gain = jnp.clip(1.0 + 0.1 * jax.random.normal(streams_of[5], (N_PIPE, D), jnp.float32), 0.5, 1.5).astype(jnp.bfloat16)
    router = gaussian(streams_of[6], (N_PIPE, D, EXPERTS), D ** -0.5, 0.09375, ((0, 4),))
    w_gate = gaussian(streams_of[7], (N_PIPE, N_EXPERT, D, FF_DEV), D ** -0.5, 0.09375, ((0, 4), (1, 64)))
    w_up = gaussian(streams_of[8], (N_PIPE, N_EXPERT, D, FF_DEV), D ** -0.5, 0.09375, ((0, 4), (1, 64)))
    w_down = gaussian(streams_of[9], (N_PIPE, N_EXPERT, FF_DEV, D), FF ** -0.5, 0.1875, ((0, 4), (1, 64)))
    return {"act_a": act_a, "ids_a": ids_a, "act_b": act_b, "cot_b": cot_b, "ids_b": ids_b, "norm_gain": norm_gain, "router": router, "w_gate": w_gate, "w_up": w_up, "w_down": w_down}


route_scale = 2.5
norm_eps = 1e-06

def normalize(inputs, gain_row):
    values = inputs.astype(jnp.float32)
    inverse = lax.rsqrt(lax.optimization_barrier(jnp.mean(values * values, axis=-1, keepdims=True)) + norm_eps)
    normed = (values * inverse * gain_row.astype(jnp.float32)).astype(jnp.bfloat16)
    return (normed, values, inverse)

def route_gates(normed, router_cols, expert_ids):
    logits = jnp.dot(normed, router_cols, preferred_element_type=jnp.float32)
    picker = expert_ids[:, :, None] == jnp.arange(router_cols.shape[1], dtype=jnp.int32)[None, None, :]
    chosen = lax.optimization_barrier(jnp.sum(jnp.where(picker, logits[:, None, :], 0.0), axis=2))
    scores = jax.nn.sigmoid(chosen)
    return (scores, scores / lax.optimization_barrier(jnp.sum(scores, axis=1, keepdims=True)), picker)

def expert_forward(rows_in, gate_w, up_w, down_w):
    gate_pre = jnp.dot(rows_in, gate_w, preferred_element_type=jnp.float32)
    up_pre = jnp.dot(rows_in, up_w, preferred_element_type=jnp.float32)
    sig_gate = jax.nn.sigmoid(gate_pre)
    activation = (gate_pre * sig_gate * up_pre).astype(jnp.bfloat16)
    output = jnp.dot(activation, down_w, preferred_element_type=jnp.float32).astype(jnp.bfloat16)
    return (output, gate_pre, up_pre, sig_gate)

def expert_backward(rows_in, grad_rows, gate_w, up_w, down_w):
    output, gate_pre, up_pre, sig_gate = expert_forward(rows_in, gate_w, up_w, down_w)
    contract = lax.optimization_barrier(jnp.sum(grad_rows.astype(jnp.float32) * output.astype(jnp.float32), axis=-1)).astype(jnp.bfloat16)
    last_dims = (((1,), (1,)), ((), ()))
    grad_act = lax.dot_general(grad_rows, down_w, last_dims, preferred_element_type=jnp.float32)
    grad_gate = (grad_act * up_pre * sig_gate * (1.0 + gate_pre * (1.0 - sig_gate))).astype(jnp.bfloat16)
    grad_up = (grad_act * gate_pre * sig_gate).astype(jnp.bfloat16)
    grad_in = lax.dot_general(grad_gate, gate_w, last_dims, preferred_element_type=jnp.float32)
    grad_in = grad_in + lax.dot_general(grad_up, up_w, last_dims, preferred_element_type=jnp.float32)
    return (grad_in.astype(jnp.bfloat16), contract)

def split_weights(gate_all, up_all, down_all):
    gate_set = gate_all.reshape(EXPERTS, SPLIT, gate_all.shape[1], gate_all.shape[2])
    up_set = up_all.reshape(EXPERTS, SPLIT, up_all.shape[1], up_all.shape[2])
    down_set = down_all.reshape(EXPERTS, SPLIT, down_all.shape[1], down_all.shape[2])
    return (gate_set, up_set, down_set)

def forward_rank(inputs, expert_ids, gain_row, router_cols, gate_all, up_all, down_all):
    normed, values, inverse = normalize(inputs, gain_row)
    scores, share, picker = route_gates(normed, router_cols, expert_ids)
    flat_ids = expert_ids.reshape(-1)
    flat_share = share.reshape(-1)
    capacity_rows = N_EXPERT * CAP
    gate_set, up_set, down_set = split_weights(gate_all, up_all, down_all)

    def one_expert(branch, packed):
        gate_w, up_w, down_w, number = packed
        matches = flat_ids == number
        picked = jnp.nonzero(matches, size=capacity_rows, fill_value=0)[0]
        is_valid = (jnp.arange(capacity_rows) < jnp.sum(matches))[:, None]
        token_rows = picked // TOP
        rows_in = normed[token_rows]
        total = jnp.zeros((capacity_rows, values.shape[1]), jnp.float32)
        for slice_index in range(SPLIT):
            part = expert_forward(rows_in, gate_w[slice_index], up_w[slice_index], down_w[slice_index])[0]
            total = total + part.astype(jnp.float32)
        weighted = jnp.where(is_valid, flat_share[picked][:, None] * total, 0.0)
        return (branch.at[token_rows].add(weighted), None)
    numbers = jnp.arange(EXPERTS, dtype=jnp.int32)
    branch = lax.scan(one_expert, jnp.zeros(values.shape, jnp.float32), (gate_set, up_set, down_set, numbers))[0]
    return (values + route_scale * branch).astype(jnp.bfloat16)

def backward_rank(inputs, grad_out, expert_ids, gain_row, router_cols, gate_all, up_all, down_all):
    normed, values, inverse = normalize(inputs, gain_row)
    scores, share, picker = route_gates(normed, router_cols, expert_ids)
    flat_ids = expert_ids.reshape(-1)
    flat_share = share.reshape(-1)
    capacity_rows = N_EXPERT * CAP
    gate_set, up_set, down_set = split_weights(gate_all, up_all, down_all)

    def one_expert(running, packed):
        branch, contracts = running
        gate_w, up_w, down_w, number = packed
        matches = flat_ids == number
        picked = jnp.nonzero(matches, size=capacity_rows, fill_value=0)[0]
        is_valid = jnp.arange(capacity_rows) < jnp.sum(matches)
        token_rows = picked // TOP
        rows_in = normed[token_rows]
        rows_grad = grad_out[token_rows]
        grad_total = jnp.zeros((capacity_rows, values.shape[1]), jnp.float32)
        contract_total = jnp.zeros((capacity_rows,), jnp.float32)
        for slice_index in range(SPLIT):
            grad_in, contract = expert_backward(rows_in, rows_grad, gate_w[slice_index], up_w[slice_index], down_w[slice_index])
            grad_total = grad_total + grad_in.astype(jnp.float32)
            contract_total = contract_total + contract.astype(jnp.float32)
        weighted = jnp.where(is_valid[:, None], flat_share[picked][:, None] * grad_total, 0.0)
        contracts = contracts.at[picked].add(jnp.where(is_valid, contract_total, 0.0))
        return ((branch.at[token_rows].add(weighted), contracts), None)
    numbers = jnp.arange(EXPERTS, dtype=jnp.int32)
    start = (jnp.zeros(values.shape, jnp.float32), jnp.zeros(flat_ids.shape, jnp.float32))
    branch, contracts = lax.scan(one_expert, start, (gate_set, up_set, down_set, numbers))[0]
    grad_share = route_scale * contracts.reshape(share.shape)
    grad_scores = (grad_share - lax.optimization_barrier(jnp.sum(share * grad_share, axis=1, keepdims=True))) / lax.optimization_barrier(jnp.sum(scores, axis=1, keepdims=True))
    grad_logit = grad_scores * scores * (1.0 - scores)
    dense_grad = lax.optimization_barrier(jnp.sum(jnp.where(picker, grad_logit[:, :, None], 0.0), axis=1)).astype(jnp.bfloat16)
    router_term = lax.dot_general(dense_grad, router_cols, (((1,), (1,)), ((), ())), preferred_element_type=jnp.float32)
    grad_normed = (route_scale * branch + router_term) * gain_row.astype(jnp.float32)
    center = lax.optimization_barrier(jnp.mean(values * grad_normed, axis=-1, keepdims=True))
    grad_values = grad_out.astype(jnp.float32) + inverse * grad_normed - values * inverse * inverse * inverse * center
    return grad_values.astype(jnp.bfloat16)

def reference(act_a, ids_a, act_b, cot_b, ids_b, norm_gain, router, w_gate, w_up, w_down):
    forward_all = []
    backward_all = []
    for section_index in range(N_PIPE):
        forward_all.append(forward_rank(act_a[section_index], ids_a[section_index], norm_gain[section_index], router[section_index], w_gate[section_index], w_up[section_index], w_down[section_index]))
        backward_all.append(backward_rank(act_b[section_index], cot_b[section_index], ids_b[section_index], norm_gain[section_index], router[section_index], w_gate[section_index], w_up[section_index], w_down[section_index]))
    next_a = jnp.roll(jnp.stack(forward_all), 1, axis=0)
    next_b = jnp.roll(jnp.stack(backward_all), -1, axis=0)
    return (next_a, next_b)
```

```python
import jax
import jax.numpy as jnp
from jax import lax
from jax.sharding import PartitionSpec as P

SPLIT = 4


route_scale = 2.5
norm_eps = 1e-06


def from_behind(array, axis, by):
    size = lax.axis_size(axis)
    return lax.ppermute(array, axis, [(i, (i + by) % size) for i in range(size)])


def with_peer(array, flip):
    size = lax.axis_size("expert")
    return lax.ppermute(array, "expert", [(i, i ^ flip) for i in range(size)])


def matmul(a, b):
    return jnp.dot(a, b, preferred_element_type=jnp.float32)


def matmul_t(a, b):
    return lax.dot_general(a, b, (((1,), (1,)), ((), ())), preferred_element_type=jnp.float32)


def normalize(inputs, gain_row):
    values = inputs.astype(jnp.float32)
    inverse = lax.rsqrt(jnp.mean(values * values, axis=-1, keepdims=True) + norm_eps)
    normed = (values * inverse * gain_row.astype(jnp.float32)).astype(jnp.bfloat16)
    return (normed, values, inverse)


def route_gates(normed, router_cols, expert_ids):
    logits = matmul(normed, router_cols)
    picker = (
        expert_ids[:, :, None] == jnp.arange(router_cols.shape[1], dtype=jnp.int32)[None, None, :]
    )
    chosen = jnp.sum(jnp.where(picker, logits[:, None, :], 0.0), axis=2)
    scores = jax.nn.sigmoid(chosen)
    return (scores, scores / jnp.sum(scores, axis=1, keepdims=True), picker)


def slot_numbers(expert_ids, experts, capacity):
    flat_ids = expert_ids.reshape(-1)
    count = flat_ids.shape[0]
    onehot = flat_ids[:, None] == jnp.arange(experts, dtype=jnp.int32)[None, :]
    earlier = jnp.arange(count)[:, None] > jnp.arange(count)[None, :]
    before = matmul(earlier.astype(jnp.bfloat16), onehot.astype(jnp.bfloat16))
    rank = jnp.sum(jnp.where(onehot, before, 0.0), axis=1).astype(jnp.int32)
    return (flat_ids * capacity + rank).reshape(expert_ids.shape)


def slot_matrix(slots, k, total):
    return (slots[:, k][:, None] == jnp.arange(total, dtype=jnp.int32)[None, :]).astype(
        jnp.bfloat16
    )


def to_blocks(rows, experts, capacity):
    width = rows.shape[1] // SPLIT
    blocks = rows.reshape(experts, capacity, SPLIT, width).transpose(0, 2, 1, 3)
    return blocks.reshape(experts * SPLIT, capacity * width // 128, 128)


def from_blocks(blocks, experts, capacity):
    width = blocks.shape[1] * 128 // capacity
    rows = blocks.reshape(experts, SPLIT, capacity, width).transpose(0, 2, 1, 3)
    return rows.reshape(experts * capacity, SPLIT * width)


def exchange(blocks):
    return lax.all_to_all(blocks, "expert", split_axis=0, concat_axis=0, tiled=True)


def per_device(act_a, ids_a, act_b, cot_b, ids_b, norm_gain, router, w_gate, w_up, w_down):
    experts = lax.axis_size("expert") // SPLIT
    token_count = act_a.shape[1]
    top_count = ids_a.shape[2]
    width = act_a.shape[2]
    quarter = width // SPLIT
    capacity = min(token_count, max(2, 5 * token_count * top_count // (4 * experts)))
    slots_total = experts * capacity
    rows_total = slots_total * SPLIT
    hidden = w_gate.shape[3]
    gain_row = norm_gain[0]
    router_cols = router[0]
    mine = lax.rem(lax.axis_index("expert"), SPLIT)

    gate_up, down = [], []
    for flip in range(SPLIT):
        start = lax.bitwise_xor(mine, flip) * quarter
        both = jnp.concatenate(
            [lax.dynamic_slice_in_dim(w[0, 0], start, quarter, 0) for w in (w_gate, w_up)], axis=1
        )
        last = lax.dynamic_slice_in_dim(w_down[0, 0], start, quarter, 1)
        if flip:
            both, last = with_peer(both, flip), with_peer(last, flip)
        gate_up.append(both)
        down.append(last)

    def pack(rows, slots):
        spread = sum(slot_matrix(slots, k, slots_total) for k in range(top_count))
        packed = lax.dot_general(
            spread, rows, (((0,), (0,)), ((), ())), preferred_element_type=jnp.float32
        )
        return to_blocks(packed.astype(jnp.bfloat16), experts, capacity)

    normed_a, values_a, inverse_a = normalize(act_a[0], gain_row)
    slots_a = slot_numbers(ids_a[0], experts, capacity)
    rows_a = exchange(pack(normed_a, slots_a)).reshape(rows_total, quarter)
    grad_out = cot_b[0]
    normed_b, values_b, inverse_b = normalize(act_b[0], gain_row)
    slots_b = slot_numbers(ids_b[0], experts, capacity)
    rows_b = exchange(pack(normed_b, slots_b)).reshape(rows_total, quarter)
    rows_c = exchange(pack(grad_out, slots_b)).reshape(rows_total, quarter)

    def summed(parts):
        total = parts[0]
        for flip in range(1, SPLIT):
            total = total + with_peer(parts[flip].astype(jnp.bfloat16), flip).astype(jnp.float32)
        return total

    def gathered(part):
        return [part] + [with_peer(part, flip) for flip in range(1, SPLIT)]

    pre_a = summed([matmul(rows_a, w) for w in gate_up])
    gate_a, up_a = pre_a[:, :hidden], pre_a[:, hidden:]
    activ_a = gathered((gate_a * jax.nn.sigmoid(gate_a) * up_a).astype(jnp.bfloat16))
    output_a = sum(matmul(a, w) for a, w in zip(activ_a, down)).astype(jnp.bfloat16)
    back_a = output_a.reshape(experts * SPLIT, capacity * quarter // 128, 128)
    home_a = from_blocks(exchange(back_a), experts, capacity)

    pre_b = summed([matmul(rows_b, w) for w in gate_up])
    grad_act = summed([matmul_t(rows_c, w) for w in down])
    gate_b, up_b = pre_b[:, :hidden], pre_b[:, hidden:]
    sig_b = jax.nn.sigmoid(gate_b)
    activ_b = (gate_b * sig_b * up_b).astype(jnp.bfloat16)
    contract = jnp.sum(activ_b.astype(jnp.float32) * grad_act, axis=1).astype(jnp.bfloat16)
    grad_gate = (grad_act * up_b * sig_b * (1.0 + gate_b * (1.0 - sig_b))).astype(jnp.bfloat16)
    grad_up = (grad_act * gate_b * sig_b).astype(jnp.bfloat16)
    grads = gathered(jnp.concatenate([grad_gate, grad_up], axis=1))
    grad_in = sum(matmul_t(g, w) for g, w in zip(grads, gate_up)).astype(jnp.bfloat16)
    back_b = grad_in.reshape(experts * SPLIT, capacity * quarter // 128, 128)
    extra = jnp.pad(contract.reshape(experts * SPLIT, 1, capacity), ((0, 0), (0, 1), (0, 128 - capacity)))
    home_b = exchange(jnp.concatenate([back_b, extra], axis=1))
    home_contract = jnp.sum(
        home_b[:, back_b.shape[1], :capacity].reshape(experts, SPLIT, capacity).astype(jnp.float32),
        axis=1,
    ).reshape(1, slots_total)
    home_grad = from_blocks(home_b[:, : back_b.shape[1]], experts, capacity)

    scores_a, share_a, picker_a = route_gates(normed_a, router_cols, ids_a[0])
    mixed_a = sum(
        share_a[:, k : k + 1] * matmul(slot_matrix(slots_a, k, slots_total), home_a)
        for k in range(top_count)
    )
    section_a = (values_a + route_scale * mixed_a).astype(jnp.bfloat16)
    next_a = from_behind(section_a[None], "pipe", 1)

    scores_b, share_b, picker_b = route_gates(normed_b, router_cols, ids_b[0])
    picks = [slot_matrix(slots_b, k, slots_total) for k in range(top_count)]
    branch_b = sum(share_b[:, k : k + 1] * matmul(picks[k], home_grad) for k in range(top_count))
    contracts = jnp.concatenate(
        [
            jnp.sum(picks[k].astype(jnp.float32) * home_contract, axis=1, keepdims=True)
            for k in range(top_count)
        ],
        axis=1,
    )
    grad_share = route_scale * contracts
    grad_scores = (grad_share - jnp.sum(share_b * grad_share, axis=1, keepdims=True)) / jnp.sum(
        scores_b, axis=1, keepdims=True
    )
    grad_logit = grad_scores * scores_b * (1.0 - scores_b)
    dense_grad = jnp.sum(jnp.where(picker_b, grad_logit[:, :, None], 0.0), axis=1).astype(
        jnp.bfloat16
    )
    router_term = matmul_t(dense_grad, router_cols)
    grad_normed = (route_scale * branch_b + router_term) * gain_row.astype(jnp.float32)
    center = jnp.mean(values_b * grad_normed, axis=-1, keepdims=True)
    grad_values = (
        grad_out.astype(jnp.float32)
        + inverse_b * grad_normed
        - values_b * inverse_b * inverse_b * inverse_b * center
    )
    next_b = from_behind(grad_values.astype(jnp.bfloat16)[None], "pipe", -1)
    return (next_a, next_b)


def solution(mesh):
    return jax.shard_map(
        per_device,
        mesh=mesh,
        in_specs=(
            P("pipe", "expert", None),
            P("pipe", "expert", None),
            P("pipe", "expert", None),
            P("pipe", "expert", None),
            P("pipe", "expert", None),
            P("pipe", None),
            P("pipe", None, None),
            P("pipe", "expert", None, None),
            P("pipe", "expert", None, None),
            P("pipe", "expert", None, None),
        ),
        out_specs=(P("pipe", "expert", None), P("pipe", "expert", None)),
        check_vma=False,
    )
```

```python
import jax
import jax.numpy as jnp
from jax import lax
from jax.sharding import PartitionSpec as P

SPLIT = 4
HALVES = 2


route_scale = 2.5
norm_eps = 1e-06


def from_behind(array, axis, by):
    size = lax.axis_size(axis)
    return lax.ppermute(array, axis, [(i, (i + by) % size) for i in range(size)])


def with_peer(array, flip):
    size = lax.axis_size("expert")
    return lax.ppermute(array, "expert", [(i, i ^ flip) for i in range(size)])


def matmul(a, b):
    return jnp.dot(a, b, preferred_element_type=jnp.float32)


def matmul_t(a, b):
    return lax.dot_general(a, b, (((1,), (1,)), ((), ())), preferred_element_type=jnp.float32)


def normalize(inputs, gain_row):
    values = inputs.astype(jnp.float32)
    inverse = lax.rsqrt(jnp.mean(values * values, axis=-1, keepdims=True) + norm_eps)
    normed = (values * inverse * gain_row.astype(jnp.float32)).astype(jnp.bfloat16)
    return (normed, values, inverse)


def route_gates(normed, router_cols, expert_ids):
    logits = matmul(normed, router_cols)
    picker = (
        expert_ids[:, :, None] == jnp.arange(router_cols.shape[1], dtype=jnp.int32)[None, None, :]
    )
    chosen = jnp.sum(jnp.where(picker, logits[:, None, :], 0.0), axis=2)
    scores = jax.nn.sigmoid(chosen)
    return (scores, scores / jnp.sum(scores, axis=1, keepdims=True), picker)


def slot_numbers(expert_ids, experts, capacity):
    flat_ids = expert_ids.reshape(-1)
    count = flat_ids.shape[0]
    onehot = flat_ids[:, None] == jnp.arange(experts, dtype=jnp.int32)[None, :]
    earlier = jnp.arange(count)[:, None] > jnp.arange(count)[None, :]
    before = matmul(earlier.astype(jnp.bfloat16), onehot.astype(jnp.bfloat16))
    rank = jnp.sum(jnp.where(onehot, before, 0.0), axis=1).astype(jnp.int32)
    return (flat_ids * capacity + rank).reshape(expert_ids.shape)


def slot_matrix(slots, k, total):
    return (slots[:, k][:, None] == jnp.arange(total, dtype=jnp.int32)[None, :]).astype(
        jnp.bfloat16
    )


def to_blocks(rows, experts, capacity):
    width = rows.shape[1] // HALVES
    blocks = rows.reshape(experts, capacity, HALVES, width).transpose(0, 2, 1, 3)
    return blocks.reshape(experts * HALVES, capacity * width // 128, 128)


def from_blocks(blocks, experts, capacity):
    width = blocks.shape[1] * 128 // capacity
    rows = blocks.reshape(experts, HALVES, capacity, width).transpose(0, 2, 1, 3)
    return rows.reshape(experts * capacity, HALVES * width)


def exchange(blocks):
    size = lax.axis_size("expert")
    groups = [list(range(low, size, 2)) for low in range(2)]
    return lax.all_to_all(
        blocks, "expert", split_axis=0, concat_axis=0, axis_index_groups=groups, tiled=True
    )


def per_device(act_a, ids_a, act_b, cot_b, ids_b, norm_gain, router, w_gate, w_up, w_down):
    experts = lax.axis_size("expert") // SPLIT
    token_count = act_a.shape[1]
    top_count = ids_a.shape[2]
    width = act_a.shape[2]
    half = width // HALVES
    capacity = min(token_count, max(2, 5 * token_count * top_count // (4 * experts)))
    slots_total = experts * capacity
    rows_total = slots_total * HALVES
    block_rows = capacity * half // 128
    hidden = w_gate.shape[3]
    pair = 2 * hidden
    gain_row = norm_gain[0]
    router_cols = router[0]
    side = lax.rem(lax.axis_index("expert") // 2, 2)

    def half_of(weight, which, axis):
        return lax.dynamic_slice_in_dim(weight[0, 0], which * half, half, axis)

    def gate_up_of(which):
        return jnp.concatenate([half_of(w_gate, which, 0), half_of(w_up, which, 0)], axis=1)

    gu_own, down_own = gate_up_of(side), half_of(w_down, side, 1)
    gu_x, down_x = with_peer(gate_up_of(1 - side), 2), with_peer(half_of(w_down, 1 - side, 1), 2)
    gu_y, down_y = with_peer(gu_own, 1), with_peer(down_own, 1)

    def pack(rows, slots):
        spread = sum(slot_matrix(slots, k, slots_total) for k in range(top_count))
        packed = lax.dot_general(
            spread, rows, (((0,), (0,)), ((), ())), preferred_element_type=jnp.float32
        )
        return to_blocks(packed.astype(jnp.bfloat16), experts, capacity)

    def as_rows(blocks):
        return blocks.reshape(rows_total, half)

    def swapped(part):
        return with_peer(part.astype(jnp.bfloat16), 2)

    normed_a, values_a, inverse_a = normalize(act_a[0], gain_row)
    slots_a = slot_numbers(ids_a[0], experts, capacity)
    rows_a = as_rows(exchange(pack(normed_a, slots_a)))
    grad_out = cot_b[0]
    normed_b, values_b, inverse_b = normalize(act_b[0], gain_row)
    slots_b = slot_numbers(ids_b[0], experts, capacity)
    blocks_b, blocks_c = pack(normed_b, slots_b), pack(grad_out, slots_b)
    blocks_b, gu_x, gu_y = lax.optimization_barrier((blocks_b, gu_x, gu_y))
    rows_b = as_rows(exchange(blocks_b))
    gu_d = with_peer(gu_x, 1)
    blocks_c, gu_d, down_x = lax.optimization_barrier((blocks_c, gu_d, down_x))
    rows_c = as_rows(exchange(blocks_c))
    down_d = with_peer(down_x, 1)

    def pre_parts(rows):
        sent = swapped(jnp.concatenate([matmul(rows, w) for w in (gu_x, gu_d)], axis=1))
        return [matmul(rows, w) for w in (gu_own, gu_y)], sent

    def pre_total(parts, sent):
        totals = [
            part + sent[:, place * pair : (place + 1) * pair].astype(jnp.float32)
            for place, part in enumerate(parts)
        ]
        return [(total[:, :hidden], total[:, hidden:]) for total in totals]

    parts_a, sent_a = pre_parts(rows_a)
    parts_b, sent_b = pre_parts(rows_b)
    activ_a = jnp.concatenate(
        [
            (gate * jax.nn.sigmoid(gate) * up).astype(jnp.bfloat16)
            for gate, up in pre_total(parts_a, sent_a)
        ],
        axis=1,
    )
    activ_x = with_peer(activ_a, 2)
    rows_c, activ_x, sent_b = lax.optimization_barrier((rows_c, activ_x, sent_b))
    output_a = (
        matmul(activ_a[:, :hidden], down_own)
        + matmul(activ_a[:, hidden:], down_y)
        + matmul(activ_x[:, :hidden], down_x)
        + matmul(activ_x[:, hidden:], down_d)
    ).astype(jnp.bfloat16)
    home_a = from_blocks(exchange(output_a.reshape(-1, block_rows, 128)), experts, capacity)

    sent_c = swapped(jnp.concatenate([matmul_t(rows_c, w) for w in (down_x, down_d)], axis=1))
    parts_c = [matmul_t(rows_c, w) for w in (down_own, down_y)]
    contract, grads = 0.0, []
    for place, (gate, up) in enumerate(pre_total(parts_b, sent_b)):
        sig = jax.nn.sigmoid(gate)
        grad_act = parts_c[place] + sent_c[:, place * hidden : (place + 1) * hidden].astype(
            jnp.float32
        )
        activation = (gate * sig * up).astype(jnp.bfloat16).astype(jnp.float32)
        contract = contract + jnp.sum(activation * grad_act, axis=1)
        grads.append((grad_act * up * sig * (1.0 + gate * (1.0 - sig))).astype(jnp.bfloat16))
        grads.append((grad_act * gate * sig).astype(jnp.bfloat16))
    grads = jnp.concatenate(grads, axis=1)
    grads_x = with_peer(grads, 2)
    grad_in = (
        matmul_t(grads[:, :pair], gu_own)
        + matmul_t(grads[:, pair:], gu_y)
        + matmul_t(grads_x[:, :pair], gu_x)
        + matmul_t(grads_x[:, pair:], gu_d)
    ).astype(jnp.bfloat16)
    extra = jnp.pad(
        contract.astype(jnp.bfloat16).reshape(-1, 1, capacity),
        ((0, 0), (0, 3), (0, 128 - capacity)),
    )
    home_b = exchange(jnp.concatenate([grad_in.reshape(-1, block_rows, 128), extra], axis=1))
    home_contract = jnp.sum(
        home_b[:, block_rows, :capacity].astype(jnp.float32).reshape(experts, HALVES, capacity),
        axis=1,
    ).reshape(1, slots_total)
    home_grad = from_blocks(home_b[:, :block_rows], experts, capacity)

    scores_a, share_a, picker_a = route_gates(normed_a, router_cols, ids_a[0])
    mixed_a = sum(
        share_a[:, k : k + 1] * matmul(slot_matrix(slots_a, k, slots_total), home_a)
        for k in range(top_count)
    )
    section_a = (values_a + route_scale * mixed_a).astype(jnp.bfloat16)
    next_a = from_behind(section_a[None], "pipe", 1)

    scores_b, share_b, picker_b = route_gates(normed_b, router_cols, ids_b[0])
    picks = [slot_matrix(slots_b, k, slots_total) for k in range(top_count)]
    branch_b = sum(share_b[:, k : k + 1] * matmul(picks[k], home_grad) for k in range(top_count))
    contracts = jnp.concatenate(
        [
            jnp.sum(picks[k].astype(jnp.float32) * home_contract, axis=1, keepdims=True)
            for k in range(top_count)
        ],
        axis=1,
    )
    grad_share = route_scale * contracts
    grad_scores = (grad_share - jnp.sum(share_b * grad_share, axis=1, keepdims=True)) / jnp.sum(
        scores_b, axis=1, keepdims=True
    )
    grad_logit = grad_scores * scores_b * (1.0 - scores_b)
    dense_grad = jnp.sum(jnp.where(picker_b, grad_logit[:, :, None], 0.0), axis=1).astype(
        jnp.bfloat16
    )
    router_term = matmul_t(dense_grad, router_cols)
    grad_normed = (route_scale * branch_b + router_term) * gain_row.astype(jnp.float32)
    center = jnp.mean(values_b * grad_normed, axis=-1, keepdims=True)
    grad_values = (
        grad_out.astype(jnp.float32)
        + inverse_b * grad_normed
        - values_b * inverse_b * inverse_b * inverse_b * center
    )
    next_b = from_behind(grad_values.astype(jnp.bfloat16)[None], "pipe", -1)
    return (next_a, next_b)


def solution(mesh):
    return jax.shard_map(
        per_device,
        mesh=mesh,
        in_specs=(
            P("pipe", "expert", None),
            P("pipe", "expert", None),
            P("pipe", "expert", None),
            P("pipe", "expert", None),
            P("pipe", "expert", None),
            P("pipe", None),
            P("pipe", None, None),
            P("pipe", "expert", None, None),
            P("pipe", "expert", None, None),
            P("pipe", "expert", None, None),
        ),
        out_specs=(P("pipe", "expert", None), P("pipe", "expert", None)),
        check_vma=False,
    )
```

```python
import jax
import jax.numpy as jnp
from jax import lax
from jax.experimental import pallas as pl
from jax.experimental.pallas import tpu as pltpu
from jax.sharding import PartitionSpec as P

SPLIT = 4
HALVES = 2
FIRST_HOLD_US = 25.0
SECOND_HOLD_US = 12.0
STEP_US = 10.0


route_scale = 2.5
norm_eps = 1e-06


def from_behind(array, axis, by):
    size = lax.axis_size(axis)
    return lax.ppermute(array, axis, [(i, (i + by) % size) for i in range(size)])


def with_peer(array, flip):
    size = lax.axis_size("expert")
    return lax.ppermute(array, "expert", [(i, i ^ flip) for i in range(size)])


def matmul(a, b):
    return jnp.dot(a, b, preferred_element_type=jnp.float32)


def matmul_t(a, b):
    return lax.dot_general(a, b, (((1,), (1,)), ((), ())), preferred_element_type=jnp.float32)


def normalize(inputs, gain_row):
    values = inputs.astype(jnp.float32)
    inverse = lax.rsqrt(jnp.mean(values * values, axis=-1, keepdims=True) + norm_eps)
    normed = (values * inverse * gain_row.astype(jnp.float32)).astype(jnp.bfloat16)
    return (normed, values, inverse)


def route_gates(normed, router_cols, expert_ids):
    logits = matmul(normed, router_cols)
    picker = (
        expert_ids[:, :, None] == jnp.arange(router_cols.shape[1], dtype=jnp.int32)[None, None, :]
    )
    chosen = jnp.sum(jnp.where(picker, logits[:, None, :], 0.0), axis=2)
    scores = jax.nn.sigmoid(chosen)
    return (scores, scores / jnp.sum(scores, axis=1, keepdims=True), picker)


def slot_numbers(expert_ids, experts, capacity):
    flat_ids = expert_ids.reshape(-1)
    count = flat_ids.shape[0]
    onehot = flat_ids[:, None] == jnp.arange(experts, dtype=jnp.int32)[None, :]
    earlier = jnp.arange(count)[:, None] > jnp.arange(count)[None, :]
    before = matmul(earlier.astype(jnp.bfloat16), onehot.astype(jnp.bfloat16))
    rank = jnp.sum(jnp.where(onehot, before, 0.0), axis=1).astype(jnp.int32)
    return (flat_ids * capacity + rank).reshape(expert_ids.shape)


def slot_matrix(slots, k, total):
    return (slots[:, k][:, None] == jnp.arange(total, dtype=jnp.int32)[None, :]).astype(
        jnp.bfloat16
    )


def exchange(blocks):
    size = lax.axis_size("expert")
    groups = [[i + 2 * half for half in range(HALVES) for i in range(low, size, SPLIT)] for low in range(2)]
    return lax.all_to_all(
        blocks, "expert", split_axis=0, concat_axis=0, axis_index_groups=groups, tiled=True
    )


def activation_kernel(mine_ref, theirs_ref, out_ref):
    hidden = out_ref.shape[1] // 2
    for place in range(2):
        parts = [pl.ds((2 * place + half) * hidden, hidden) for half in range(2)]
        gate, up = [mine_ref[:, p] + theirs_ref[:, p].astype(jnp.float32) for p in parts]
        out_ref[:, pl.ds(place * hidden, hidden)] = (gate * jax.nn.sigmoid(gate) * up).astype(
            jnp.bfloat16
        )


def gradient_kernel(mine_ref, theirs_ref, my_grads_ref, their_grads_ref, out_ref, contract_ref):
    hidden = out_ref.shape[1] // 4
    contract = 0.0
    for place in range(2):
        parts = [pl.ds((2 * place + half) * hidden, hidden) for half in range(2)]
        span = pl.ds(place * hidden, hidden)
        gate, up = [mine_ref[:, p] + theirs_ref[:, p].astype(jnp.float32) for p in parts]
        grad_act = my_grads_ref[:, span] + their_grads_ref[:, span].astype(jnp.float32)
        sig = jax.nn.sigmoid(gate)
        activ = (gate * sig * up).astype(jnp.bfloat16).astype(jnp.float32)
        contract = contract + jnp.sum(activ * grad_act, axis=1, keepdims=True)
        grad_gate = grad_act * up * sig * (1.0 + gate * (1.0 - sig))
        out_ref[:, parts[0]] = grad_gate.astype(jnp.bfloat16)
        out_ref[:, parts[1]] = (grad_act * gate * sig).astype(jnp.bfloat16)
    contract_ref[...] = contract


def elementwise(kernel, blocks, out_shape):
    return pl.pallas_call(
        kernel,
        out_shape=out_shape,
        in_specs=[pl.BlockSpec(memory_space=pltpu.VMEM)] * len(blocks),
        out_specs=[pl.BlockSpec(memory_space=pltpu.VMEM)] * len(out_shape),
        compiler_params=pltpu.CompilerParams(vmem_limit_bytes=40 * 1024 * 1024),
        cost_estimate=pl.CostEstimate(
            flops=int(STEP_US * 1.1e9),
            bytes_accessed=int(STEP_US * 3.6e6),
            transcendentals=0,
        ),
    )(*blocks)


def hold_kernel(*refs):
    refs[-1][...] = jnp.zeros_like(refs[-1])


def hold(cost, *arrays):
    return pl.pallas_call(
        hold_kernel,
        out_shape=jax.ShapeDtypeStruct((8, 128), jnp.float32),
        in_specs=[pl.BlockSpec(memory_space=pl.ANY)] * len(arrays),
        out_specs=pl.BlockSpec(memory_space=pltpu.VMEM),
        cost_estimate=pl.CostEstimate(
            flops=int(cost * 1.1e9), bytes_accessed=int(cost * 3.6e6), transcendentals=0
        ),
    )(*arrays)


def per_device(act_a, ids_a, act_b, cot_b, ids_b, norm_gain, router, w_gate, w_up, w_down):
    experts = lax.axis_size("expert") // SPLIT
    token_count = act_a.shape[1]
    top_count = ids_a.shape[2]
    width = act_a.shape[2]
    half = width // HALVES
    capacity = min(token_count, max(2, 5 * token_count * top_count // (4 * experts)))
    slots_total = experts * capacity
    rows_total = slots_total * HALVES
    block_rows = capacity * half // 128
    hidden = w_gate.shape[3]
    pair = 2 * hidden
    gain_row = norm_gain[0]
    router_cols = router[0]
    side = lax.rem(lax.axis_index("expert") // 2, 2)

    def half_of(weight, which, axis):
        return lax.dynamic_slice_in_dim(weight[0, 0], which * half, half, axis)

    def gate_up_of(which):
        return jnp.concatenate([half_of(w_gate, which, 0), half_of(w_up, which, 0)], axis=1)

    gu_own, down_own = gate_up_of(side), half_of(w_down, side, 1)
    gu_x, gu_y = with_peer(gate_up_of(1 - side), 2), with_peer(gu_own, 1)
    gu_x, down_given = lax.optimization_barrier((gu_x, half_of(w_down, 1 - side, 1)))
    gu_d, down_x = with_peer(gu_x, 1), with_peer(down_given, 2)
    gu_d, down_kept = lax.optimization_barrier((gu_d, down_own))
    down_y = with_peer(down_kept, 1)

    def pack(rows, slots):
        spread = sum(slot_matrix(slots, k, slots_total) for k in range(top_count))
        blocks = []
        for start in range(0, width, half):
            packed = lax.dot_general(
                spread,
                rows[:, start : start + half],
                (((0,), (0,)), ((), ())),
                preferred_element_type=jnp.float32,
            )
            blocks.append(packed.astype(jnp.bfloat16).reshape(experts, block_rows, 128))
        return jnp.concatenate(blocks, axis=0)

    def unpack(blocks):
        halves = blocks.reshape(HALVES, slots_total, half)
        return jnp.concatenate([halves[0], halves[1]], axis=1)

    def as_rows(blocks):
        return blocks.reshape(rows_total, half)

    def swapped(part):
        return with_peer(part.astype(jnp.bfloat16), 2)

    normed_a, values_a, inverse_a = normalize(act_a[0], gain_row)
    slots_a = slot_numbers(ids_a[0], experts, capacity)
    blocks_a, _ = lax.optimization_barrier((pack(normed_a, slots_a), gu_own))
    rows_a = as_rows(exchange(blocks_a))
    grad_out = cot_b[0]
    normed_b, values_b, inverse_b = normalize(act_b[0], gain_row)
    slots_b = slot_numbers(ids_b[0], experts, capacity)
    blocks_b, blocks_c = pack(normed_b, slots_b), pack(grad_out, slots_b)
    zeros_b = hold(FIRST_HOLD_US, gu_x, gu_y)
    blocks_b, zeros_b = lax.optimization_barrier((blocks_b, zeros_b))
    rows_b = as_rows(exchange(blocks_b))
    zeros_c = hold(SECOND_HOLD_US, gu_d)
    blocks_c, zeros_c = lax.optimization_barrier((blocks_c, zeros_c))
    rows_c = as_rows(exchange(blocks_c))
    down_d = with_peer(down_x, 1)

    def pre_parts(rows):
        sent = swapped(jnp.concatenate([matmul(rows, w) for w in (gu_x, gu_d)], axis=1))
        return jnp.concatenate([matmul(rows, w) for w in (gu_own, gu_y)], axis=1), sent

    mine_a, sent_a = pre_parts(rows_a)
    mine_b, sent_b = pre_parts(rows_b)
    (activ_a,) = elementwise(
        activation_kernel,
        (mine_a, sent_a),
        [jax.ShapeDtypeStruct((rows_total, pair), jnp.bfloat16)],
    )
    activ_x = with_peer(activ_a, 2)
    rows_c, activ_x, sent_b = lax.optimization_barrier((rows_c, activ_x, sent_b))
    output_a = (
        matmul(activ_a[:, :hidden], down_own)
        + matmul(activ_a[:, hidden:], down_y)
        + matmul(activ_x[:, :hidden], down_x)
        + matmul(activ_x[:, hidden:], down_d)
    ).astype(jnp.bfloat16)
    home_a = unpack(exchange(output_a.reshape(-1, block_rows, 128)))

    sent_c = swapped(jnp.concatenate([matmul_t(rows_c, w) for w in (down_x, down_d)], axis=1))
    mine_c = jnp.concatenate([matmul_t(rows_c, w) for w in (down_own, down_y)], axis=1)
    grads, contract = elementwise(
        gradient_kernel,
        (mine_b, sent_b, mine_c, sent_c),
        [
            jax.ShapeDtypeStruct((rows_total, 2 * pair), jnp.bfloat16),
            jax.ShapeDtypeStruct((rows_total, 1), jnp.float32),
        ],
    )
    grads_x = with_peer(grads, 2)
    grad_in = (
        matmul_t(grads[:, :pair], gu_own)
        + matmul_t(grads[:, pair:], gu_y)
        + matmul_t(grads_x[:, :pair], gu_x)
        + matmul_t(grads_x[:, pair:], gu_d)
    ).astype(jnp.bfloat16)
    extra = jnp.pad(
        (contract + zeros_b[0, 0] + zeros_c[0, 0]).astype(jnp.bfloat16).reshape(-1, 1, capacity),
        ((0, 0), (0, 3), (0, 128 - capacity)),
    )
    home_b = exchange(jnp.concatenate([grad_in.reshape(-1, block_rows, 128), extra], axis=1))
    home_contract = jnp.sum(
        home_b[:, block_rows, :capacity].astype(jnp.float32).reshape(HALVES, experts, capacity),
        axis=0,
    ).reshape(1, slots_total)
    home_grad = unpack(home_b[:, :block_rows])

    scores_a, share_a, picker_a = route_gates(normed_a, router_cols, ids_a[0])
    mixed_a = sum(
        share_a[:, k : k + 1] * matmul(slot_matrix(slots_a, k, slots_total), home_a)
        for k in range(top_count)
    )
    section_a = (values_a + route_scale * mixed_a).astype(jnp.bfloat16)
    next_a = from_behind(section_a[None], "pipe", 1)

    scores_b, share_b, picker_b = route_gates(normed_b, router_cols, ids_b[0])
    picks = [slot_matrix(slots_b, k, slots_total) for k in range(top_count)]
    branch_b = sum(share_b[:, k : k + 1] * matmul(picks[k], home_grad) for k in range(top_count))
    contracts = jnp.concatenate(
        [
            jnp.sum(picks[k].astype(jnp.float32) * home_contract, axis=1, keepdims=True)
            for k in range(top_count)
        ],
        axis=1,
    )
    grad_share = route_scale * contracts
    grad_scores = (grad_share - jnp.sum(share_b * grad_share, axis=1, keepdims=True)) / jnp.sum(
        scores_b, axis=1, keepdims=True
    )
    grad_logit = grad_scores * scores_b * (1.0 - scores_b)
    dense_grad = jnp.sum(jnp.where(picker_b, grad_logit[:, :, None], 0.0), axis=1).astype(
        jnp.bfloat16
    )
    router_term = matmul_t(dense_grad, router_cols)
    grad_normed = (route_scale * branch_b + router_term) * gain_row.astype(jnp.float32)
    center = jnp.mean(values_b * grad_normed, axis=-1, keepdims=True)
    grad_values = (
        grad_out.astype(jnp.float32)
        + inverse_b * grad_normed
        - values_b * inverse_b * inverse_b * inverse_b * center
    )
    next_b = from_behind(grad_values.astype(jnp.bfloat16)[None], "pipe", -1)
    return (next_a, next_b)


def solution(mesh):
    return jax.shard_map(
        per_device,
        mesh=mesh,
        in_specs=(
            P("pipe", "expert", None),
            P("pipe", "expert", None),
            P("pipe", "expert", None),
            P("pipe", "expert", None),
            P("pipe", "expert", None),
            P("pipe", None),
            P("pipe", None, None),
            P("pipe", "expert", None, None),
            P("pipe", "expert", None, None),
            P("pipe", "expert", None, None),
        ),
        out_specs=(P("pipe", "expert", None), P("pipe", "expert", None)),
        check_vma=False,
    )
```

```python
import jax
import jax.numpy as jnp
from jax import lax
from jax.experimental import pallas as pl
from jax.experimental.pallas import tpu as pltpu
from jax.sharding import PartitionSpec as P

SPLIT = 4
HALVES = 2
FIRST_HOLD_US = 25.0
SECOND_HOLD_US = 12.0
STEP_US = 10.0


route_scale = 2.5
norm_eps = 1e-06


def from_behind(array, axis, by):
    size = lax.axis_size(axis)
    return lax.ppermute(array, axis, [(i, (i + by) % size) for i in range(size)])


def with_peer(array, flip):
    size = lax.axis_size("expert")
    return lax.ppermute(array, "expert", [(i, i ^ flip) for i in range(size)])


def matmul(a, b):
    return jnp.dot(a, b, preferred_element_type=jnp.float32)


def matmul_t(a, b):
    return lax.dot_general(a, b, (((1,), (1,)), ((), ())), preferred_element_type=jnp.float32)


def normalize(inputs, gain_row):
    values = inputs.astype(jnp.float32)
    inverse = lax.rsqrt(jnp.mean(values * values, axis=-1, keepdims=True) + norm_eps)
    normed = (values * inverse * gain_row.astype(jnp.float32)).astype(jnp.bfloat16)
    return (normed, values, inverse)


def route_gates(normed, router_cols, expert_ids):
    logits = matmul(normed, router_cols)
    picker = (
        expert_ids[:, :, None] == jnp.arange(router_cols.shape[1], dtype=jnp.int32)[None, None, :]
    )
    chosen = jnp.sum(jnp.where(picker, logits[:, None, :], 0.0), axis=2)
    scores = jax.nn.sigmoid(chosen)
    return (scores, scores / jnp.sum(scores, axis=1, keepdims=True), picker)


def slot_numbers(expert_ids, experts, capacity):
    flat_ids = expert_ids.reshape(-1)
    count = flat_ids.shape[0]
    onehot = flat_ids[:, None] == jnp.arange(experts, dtype=jnp.int32)[None, :]
    earlier = jnp.arange(count)[:, None] > jnp.arange(count)[None, :]
    before = matmul(earlier.astype(jnp.bfloat16), onehot.astype(jnp.bfloat16))
    rank = jnp.sum(jnp.where(onehot, before, 0.0), axis=1).astype(jnp.int32)
    return (flat_ids * capacity + rank).reshape(expert_ids.shape)


def slot_matrix(slots, k, total):
    return (slots[:, k][:, None] == jnp.arange(total, dtype=jnp.int32)[None, :]).astype(
        jnp.bfloat16
    )


def exchange(blocks):
    size = lax.axis_size("expert")
    groups = [[i + 2 * half for half in range(HALVES) for i in range(low, size, SPLIT)] for low in range(2)]
    return lax.all_to_all(
        blocks, "expert", split_axis=0, concat_axis=0, axis_index_groups=groups, tiled=True
    )


def activation_kernel(mine_ref, theirs_ref, out_ref):
    hidden = out_ref.shape[1] // 2
    for place in range(2):
        parts = [pl.ds((2 * place + half) * hidden, hidden) for half in range(2)]
        gate, up = [mine_ref[:, p] + theirs_ref[:, p].astype(jnp.float32) for p in parts]
        out_ref[:, pl.ds(place * hidden, hidden)] = (gate * jax.nn.sigmoid(gate) * up).astype(
            jnp.bfloat16
        )


def gradient_kernel(mine_ref, theirs_ref, my_grads_ref, their_grads_ref, out_ref, contract_ref):
    hidden = out_ref.shape[1] // 4
    contract = 0.0
    for place in range(2):
        parts = [pl.ds((2 * place + half) * hidden, hidden) for half in range(2)]
        span = pl.ds(place * hidden, hidden)
        gate, up = [mine_ref[:, p] + theirs_ref[:, p].astype(jnp.float32) for p in parts]
        grad_act = my_grads_ref[:, span] + their_grads_ref[:, span].astype(jnp.float32)
        sig = jax.nn.sigmoid(gate)
        activ = (gate * sig * up).astype(jnp.bfloat16).astype(jnp.float32)
        contract = contract + jnp.sum(activ * grad_act, axis=1, keepdims=True)
        grad_gate = grad_act * up * sig * (1.0 + gate * (1.0 - sig))
        out_ref[:, parts[0]] = grad_gate.astype(jnp.bfloat16)
        out_ref[:, parts[1]] = (grad_act * gate * sig).astype(jnp.bfloat16)
    contract_ref[...] = contract


def elementwise(kernel, blocks, out_shape):
    return pl.pallas_call(
        kernel,
        out_shape=out_shape,
        in_specs=[pl.BlockSpec(memory_space=pltpu.VMEM)] * len(blocks),
        out_specs=[pl.BlockSpec(memory_space=pltpu.VMEM)] * len(out_shape),
        compiler_params=pltpu.CompilerParams(vmem_limit_bytes=40 * 1024 * 1024),
        cost_estimate=pl.CostEstimate(
            flops=int(STEP_US * 1.1e9),
            bytes_accessed=int(STEP_US * 3.6e6),
            transcendentals=0,
        ),
    )(*blocks)


def hold_kernel(*refs):
    refs[-1][...] = jnp.zeros_like(refs[-1])


def hold(cost, *arrays):
    return pl.pallas_call(
        hold_kernel,
        out_shape=jax.ShapeDtypeStruct((8, 128), jnp.float32),
        in_specs=[pl.BlockSpec(memory_space=pl.ANY)] * len(arrays),
        out_specs=pl.BlockSpec(memory_space=pltpu.VMEM),
        cost_estimate=pl.CostEstimate(
            flops=int(cost * 1.1e9), bytes_accessed=int(cost * 3.6e6), transcendentals=0
        ),
    )(*arrays)


def per_device(act_a, ids_a, act_b, cot_b, ids_b, norm_gain, router, w_gate, w_up, w_down):
    experts = lax.axis_size("expert") // SPLIT
    token_count = act_a.shape[1]
    top_count = ids_a.shape[2]
    width = act_a.shape[2]
    half = width // HALVES
    capacity = min(token_count, max(2, 5 * token_count * top_count // (4 * experts)))
    slots_total = experts * capacity
    rows_total = slots_total * HALVES
    block_rows = capacity * half // 128
    hidden = w_gate.shape[3]
    pair = 2 * hidden
    gain_row = norm_gain[0]
    router_cols = router[0]
    side = lax.rem(lax.axis_index("expert") // 2, 2)

    def half_of(weight, which, axis):
        return lax.dynamic_slice_in_dim(weight[0, 0], which * half, half, axis)

    def gate_up_of(which):
        return jnp.concatenate([half_of(w_gate, which, 0), half_of(w_up, which, 0)], axis=1)

    gu_own, down_own = gate_up_of(side), half_of(w_down, side, 1)
    gu_x, gu_y = with_peer(gate_up_of(1 - side), 2), with_peer(gu_own, 1)
    gu_x, down_given = lax.optimization_barrier((gu_x, half_of(w_down, 1 - side, 1)))
    gu_d, down_x = with_peer(gu_x, 1), with_peer(down_given, 2)
    gu_d, down_kept = lax.optimization_barrier((gu_d, down_own))
    down_y = with_peer(down_kept, 1)

    def pack(rows, slots):
        spread = sum(slot_matrix(slots, k, slots_total) for k in range(top_count))
        blocks = []
        for start in range(0, width, half):
            packed = lax.dot_general(
                spread,
                rows[:, start : start + half],
                (((0,), (0,)), ((), ())),
                preferred_element_type=jnp.float32,
            )
            blocks.append(packed.astype(jnp.bfloat16).reshape(experts, block_rows, 128))
        return jnp.concatenate(blocks, axis=0)

    def unpack(blocks):
        return [
            blocks[place * experts : (place + 1) * experts].reshape(slots_total, half)
            for place in range(HALVES)
        ]

    def picked(matrix, halves):
        return jnp.concatenate([matmul(matrix, rows) for rows in halves], axis=1)

    def as_rows(blocks):
        return blocks.reshape(rows_total, half)

    def swapped(part):
        return with_peer(part.astype(jnp.bfloat16), 2)

    normed_a, values_a, inverse_a = normalize(act_a[0], gain_row)
    slots_a = slot_numbers(ids_a[0], experts, capacity)
    blocks_a, _ = lax.optimization_barrier((pack(normed_a, slots_a), gu_own))
    rows_a = as_rows(exchange(blocks_a))
    grad_out = cot_b[0]
    normed_b, values_b, inverse_b = normalize(act_b[0], gain_row)
    slots_b = slot_numbers(ids_b[0], experts, capacity)
    blocks_b, blocks_c = pack(normed_b, slots_b), pack(grad_out, slots_b)
    zeros_b = hold(FIRST_HOLD_US, gu_x, gu_y)
    blocks_b, zeros_b = lax.optimization_barrier((blocks_b, zeros_b))
    rows_b = as_rows(exchange(blocks_b))
    zeros_c = hold(SECOND_HOLD_US, gu_d)
    blocks_c, zeros_c = lax.optimization_barrier((blocks_c, zeros_c))
    rows_c = as_rows(exchange(blocks_c))
    down_d = with_peer(down_x, 1)

    def theirs_of(rows):
        return jnp.concatenate([matmul(rows, w) for w in (gu_x, gu_d)], axis=1).astype(
            jnp.bfloat16
        )

    def mine_of(rows):
        return jnp.concatenate([matmul(rows, w) for w in (gu_own, gu_y)], axis=1)

    sent_a, mine_a = with_peer(theirs_of(rows_a), 2), mine_of(rows_a)
    sent_b, mine_b = theirs_of(rows_b), mine_of(rows_b)
    (activ_a,) = elementwise(
        activation_kernel,
        (mine_a, sent_a),
        [jax.ShapeDtypeStruct((rows_total, pair), jnp.bfloat16)],
    )
    activ_x = with_peer(activ_a, 2)
    sent_b, _ = lax.optimization_barrier((sent_b, activ_a))
    sent_b = with_peer(sent_b, 2)
    output_a = (
        matmul(activ_a[:, :hidden], down_own)
        + matmul(activ_a[:, hidden:], down_y)
        + matmul(activ_x[:, :hidden], down_x)
        + matmul(activ_x[:, hidden:], down_d)
    ).astype(jnp.bfloat16)
    home_a = unpack(exchange(output_a.reshape(-1, block_rows, 128)))

    sent_c = swapped(jnp.concatenate([matmul_t(rows_c, w) for w in (down_x, down_d)], axis=1))
    mine_c = jnp.concatenate([matmul_t(rows_c, w) for w in (down_own, down_y)], axis=1)
    grads, contract = elementwise(
        gradient_kernel,
        (mine_b, sent_b, mine_c, sent_c),
        [
            jax.ShapeDtypeStruct((rows_total, 2 * pair), jnp.bfloat16),
            jax.ShapeDtypeStruct((rows_total, 1), jnp.float32),
        ],
    )
    grads_x = with_peer(grads, 2)
    grad_in = (
        matmul_t(grads[:, :pair], gu_own)
        + matmul_t(grads[:, pair:], gu_y)
        + matmul_t(grads_x[:, :pair], gu_x)
        + matmul_t(grads_x[:, pair:], gu_d)
    ).astype(jnp.bfloat16)
    extra = jnp.pad(
        (contract + zeros_b[0, 0] + zeros_c[0, 0]).astype(jnp.bfloat16).reshape(-1, 1, capacity),
        ((0, 0), (0, 3), (0, 128 - capacity)),
    )
    home_b = exchange(jnp.concatenate([grad_in.reshape(-1, block_rows, 128), extra], axis=1))
    home_contract = jnp.sum(
        home_b[:, block_rows, :capacity].astype(jnp.float32).reshape(HALVES, experts, capacity),
        axis=0,
    ).reshape(1, slots_total)
    home_grad = unpack(home_b[:, :block_rows])

    scores_a, share_a, picker_a = route_gates(normed_a, router_cols, ids_a[0])
    mixed_a = sum(
        share_a[:, k : k + 1] * picked(slot_matrix(slots_a, k, slots_total), home_a)
        for k in range(top_count)
    )
    section_a = (values_a + route_scale * mixed_a).astype(jnp.bfloat16)
    next_a = from_behind(section_a[None], "pipe", 1)

    scores_b, share_b, picker_b = route_gates(normed_b, router_cols, ids_b[0])
    picks = [slot_matrix(slots_b, k, slots_total) for k in range(top_count)]
    branch_b = sum(share_b[:, k : k + 1] * picked(picks[k], home_grad) for k in range(top_count))
    contracts = jnp.concatenate(
        [
            jnp.sum(picks[k].astype(jnp.float32) * home_contract, axis=1, keepdims=True)
            for k in range(top_count)
        ],
        axis=1,
    )
    grad_share = route_scale * contracts
    grad_scores = (grad_share - jnp.sum(share_b * grad_share, axis=1, keepdims=True)) / jnp.sum(
        scores_b, axis=1, keepdims=True
    )
    grad_logit = grad_scores * scores_b * (1.0 - scores_b)
    dense_grad = jnp.sum(jnp.where(picker_b, grad_logit[:, :, None], 0.0), axis=1).astype(
        jnp.bfloat16
    )
    router_term = matmul_t(dense_grad, router_cols)
    grad_normed = (route_scale * branch_b + router_term) * gain_row.astype(jnp.float32)
    center = jnp.mean(values_b * grad_normed, axis=-1, keepdims=True)
    grad_values = (
        grad_out.astype(jnp.float32)
        + inverse_b * grad_normed
        - values_b * inverse_b * inverse_b * inverse_b * center
    )
    next_b = from_behind(grad_values.astype(jnp.bfloat16)[None], "pipe", -1)
    return (next_a, next_b)


def solution(mesh):
    return jax.shard_map(
        per_device,
        mesh=mesh,
        in_specs=(
            P("pipe", "expert", None),
            P("pipe", "expert", None),
            P("pipe", "expert", None),
            P("pipe", "expert", None),
            P("pipe", "expert", None),
            P("pipe", None),
            P("pipe", None, None),
            P("pipe", "expert", None, None),
            P("pipe", "expert", None, None),
            P("pipe", "expert", None, None),
        ),
        out_specs=(P("pipe", "expert", None), P("pipe", "expert", None)),
        check_vma=False,
    )
```

```python
import jax
import jax.numpy as jnp
from jax import lax
from jax.experimental import pallas as pl
from jax.experimental.pallas import tpu as pltpu
from jax.sharding import PartitionSpec as P

SPLIT = 4
HALVES = 2
FIRST_HOLD_US = 25.0
SECOND_HOLD_US = 12.0
STEP_US = 10.0


route_scale = 2.5
norm_eps = 1e-06


def from_behind(array, axis, by):
    size = lax.axis_size(axis)
    return lax.ppermute(array, axis, [(i, (i + by) % size) for i in range(size)])


def with_peer(array, flip):
    size = lax.axis_size("expert")
    return lax.ppermute(array, "expert", [(i, i ^ flip) for i in range(size)])


def matmul(a, b):
    return jnp.dot(a, b, preferred_element_type=jnp.float32)


def matmul_t(a, b):
    return lax.dot_general(a, b, (((1,), (1,)), ((), ())), preferred_element_type=jnp.float32)


def normalize(inputs, gain_row):
    values = inputs.astype(jnp.float32)
    inverse = lax.rsqrt(jnp.mean(values * values, axis=-1, keepdims=True) + norm_eps)
    normed = (values * inverse * gain_row.astype(jnp.float32)).astype(jnp.bfloat16)
    return (normed, values, inverse)


def route_gates(normed, router_cols, expert_ids):
    logits = matmul(normed, router_cols)
    picker = (
        expert_ids[:, :, None] == jnp.arange(router_cols.shape[1], dtype=jnp.int32)[None, None, :]
    )
    chosen = jnp.sum(jnp.where(picker, logits[:, None, :], 0.0), axis=2)
    scores = jax.nn.sigmoid(chosen)
    return (scores, scores / jnp.sum(scores, axis=1, keepdims=True), picker)


def slot_numbers(expert_ids, experts, capacity):
    flat_ids = expert_ids.reshape(-1)
    count = flat_ids.shape[0]
    onehot = flat_ids[:, None] == jnp.arange(experts, dtype=jnp.int32)[None, :]
    earlier = jnp.arange(count)[:, None] > jnp.arange(count)[None, :]
    before = matmul(earlier.astype(jnp.bfloat16), onehot.astype(jnp.bfloat16))
    rank = jnp.sum(jnp.where(onehot, before, 0.0), axis=1).astype(jnp.int32)
    return (flat_ids * capacity + rank).reshape(expert_ids.shape)


def slot_matrix(slots, k, total):
    return (slots[:, k][:, None] == jnp.arange(total, dtype=jnp.int32)[None, :]).astype(
        jnp.bfloat16
    )


def exchange(blocks):
    size = lax.axis_size("expert")
    groups = [[i + 2 * half for half in range(HALVES) for i in range(low, size, SPLIT)] for low in range(2)]
    return lax.all_to_all(
        blocks, "expert", split_axis=0, concat_axis=0, axis_index_groups=groups, tiled=True
    )


def activation_kernel(mine_ref, theirs_ref, out_ref):
    hidden = out_ref.shape[1] // 2
    for place in range(2):
        parts = [pl.ds((2 * place + half) * hidden, hidden) for half in range(2)]
        gate, up = [mine_ref[:, p] + theirs_ref[:, p].astype(jnp.float32) for p in parts]
        out_ref[:, pl.ds(place * hidden, hidden)] = (gate * jax.nn.sigmoid(gate) * up).astype(
            jnp.bfloat16
        )


def gradient_kernel(mine_ref, theirs_ref, my_grads_ref, their_grads_ref, out_ref, contract_ref):
    hidden = out_ref.shape[1] // 4
    contract = 0.0
    for place in range(2):
        parts = [pl.ds((2 * place + half) * hidden, hidden) for half in range(2)]
        span = pl.ds(place * hidden, hidden)
        gate, up = [mine_ref[:, p] + theirs_ref[:, p].astype(jnp.float32) for p in parts]
        grad_act = my_grads_ref[:, span] + their_grads_ref[:, span].astype(jnp.float32)
        sig = jax.nn.sigmoid(gate)
        activ = (gate * sig * up).astype(jnp.bfloat16).astype(jnp.float32)
        contract = contract + jnp.sum(activ * grad_act, axis=1, keepdims=True)
        grad_gate = grad_act * up * sig * (1.0 + gate * (1.0 - sig))
        out_ref[:, parts[0]] = grad_gate.astype(jnp.bfloat16)
        out_ref[:, parts[1]] = (grad_act * gate * sig).astype(jnp.bfloat16)
    contract_ref[...] = contract


def elementwise(kernel, blocks, out_shape):
    return pl.pallas_call(
        kernel,
        out_shape=out_shape,
        in_specs=[pl.BlockSpec(memory_space=pltpu.VMEM)] * len(blocks),
        out_specs=[pl.BlockSpec(memory_space=pltpu.VMEM)] * len(out_shape),
        compiler_params=pltpu.CompilerParams(vmem_limit_bytes=40 * 1024 * 1024),
        cost_estimate=pl.CostEstimate(
            flops=int(STEP_US * 1.1e9),
            bytes_accessed=int(STEP_US * 3.6e6),
            transcendentals=0,
        ),
    )(*blocks)


def hold_kernel(*refs):
    refs[-1][...] = jnp.zeros_like(refs[-1])


def hold(cost, *arrays):
    return pl.pallas_call(
        hold_kernel,
        out_shape=jax.ShapeDtypeStruct((8, 128), jnp.float32),
        in_specs=[pl.BlockSpec(memory_space=pl.ANY)] * len(arrays),
        out_specs=pl.BlockSpec(memory_space=pltpu.VMEM),
        cost_estimate=pl.CostEstimate(
            flops=int(cost * 1.1e9), bytes_accessed=int(cost * 3.6e6), transcendentals=0
        ),
    )(*arrays)


def per_device(act_a, ids_a, act_b, cot_b, ids_b, norm_gain, router, w_gate, w_up, w_down):
    experts = lax.axis_size("expert") // SPLIT
    token_count = act_a.shape[1]
    top_count = ids_a.shape[2]
    width = act_a.shape[2]
    half = width // HALVES
    capacity = min(token_count, max(2, 5 * token_count * top_count // (4 * experts)))
    slots_total = experts * capacity
    rows_total = slots_total * HALVES
    block_rows = capacity * half // 128
    hidden = w_gate.shape[3]
    pair = 2 * hidden
    gain_row = norm_gain[0]
    router_cols = router[0]
    side = lax.rem(lax.axis_index("expert") // 2, 2)

    def half_of(weight, which, axis):
        return lax.dynamic_slice_in_dim(weight[0, 0], which * half, half, axis)

    def gate_up_of(which):
        return jnp.concatenate([half_of(w_gate, which, 0), half_of(w_up, which, 0)], axis=1)

    gu_own, down_own = gate_up_of(side), half_of(w_down, side, 1)
    gu_x, gu_y = with_peer(gate_up_of(1 - side), 2), with_peer(gu_own, 1)
    gu_x, down_given = lax.optimization_barrier((gu_x, half_of(w_down, 1 - side, 1)))
    gu_d, down_x = with_peer(gu_x, 1), with_peer(down_given, 2)
    gu_d, down_kept = lax.optimization_barrier((gu_d, down_own))
    down_y = with_peer(down_kept, 1)

    def pack(rows, slots):
        spread = sum(slot_matrix(slots, k, slots_total) for k in range(top_count))
        blocks = []
        for start in range(0, width, half):
            packed = lax.dot_general(
                spread,
                rows[:, start : start + half],
                (((0,), (0,)), ((), ())),
                preferred_element_type=jnp.float32,
            )
            blocks.append(packed.astype(jnp.bfloat16).reshape(experts, block_rows, 128))
        return jnp.concatenate(blocks, axis=0)

    def unpack(blocks):
        return [
            blocks[place * experts : (place + 1) * experts].reshape(slots_total, half)
            for place in range(HALVES)
        ]

    def picked(matrix, halves):
        return jnp.concatenate([matmul(matrix, rows) for rows in halves], axis=1)

    def as_rows(blocks):
        return blocks.reshape(rows_total, half)

    def swapped(part):
        return with_peer(part.astype(jnp.bfloat16), 2)

    normed_a, values_a, inverse_a = normalize(act_a[0], gain_row)
    slots_a = slot_numbers(ids_a[0], experts, capacity)
    blocks_a, _ = lax.optimization_barrier((pack(normed_a, slots_a), gu_own))
    rows_a = as_rows(exchange(blocks_a))
    grad_out = cot_b[0]
    normed_b, values_b, inverse_b = normalize(act_b[0], gain_row)
    slots_b = slot_numbers(ids_b[0], experts, capacity)
    blocks_b, blocks_c = pack(normed_b, slots_b), pack(grad_out, slots_b)
    zeros_b = hold(FIRST_HOLD_US, gu_x, gu_y)
    blocks_b, zeros_b = lax.optimization_barrier((blocks_b, zeros_b))
    rows_b = as_rows(exchange(blocks_b))
    zeros_c = hold(SECOND_HOLD_US, gu_d)
    blocks_c, zeros_c = lax.optimization_barrier((blocks_c, zeros_c))
    rows_c = as_rows(exchange(blocks_c))
    down_d = with_peer(down_x, 1)

    def theirs_of(rows):
        return jnp.concatenate([matmul(rows, w) for w in (gu_x, gu_d)], axis=1).astype(
            jnp.bfloat16
        )

    def mine_of(rows):
        return jnp.concatenate([matmul(rows, w) for w in (gu_own, gu_y)], axis=1)

    sent_a, mine_a = with_peer(theirs_of(rows_a), 2), mine_of(rows_a)
    sent_b, mine_b = theirs_of(rows_b), mine_of(rows_b)
    (activ_a,) = elementwise(
        activation_kernel,
        (mine_a, sent_a),
        [jax.ShapeDtypeStruct((rows_total, pair), jnp.bfloat16)],
    )
    activ_x = with_peer(activ_a, 2)
    sent_b, _ = lax.optimization_barrier((sent_b, activ_a))
    sent_b = with_peer(sent_b, 2)
    output_a = (
        matmul(activ_a[:, :hidden], down_own)
        + matmul(activ_a[:, hidden:], down_y)
        + matmul(activ_x[:, :hidden], down_x)
        + matmul(activ_x[:, hidden:], down_d)
    ).astype(jnp.bfloat16)
    output_a, rows_c = lax.optimization_barrier((output_a, rows_c))
    home_a = unpack(exchange(output_a.reshape(-1, block_rows, 128)))

    sent_c = swapped(jnp.concatenate([matmul_t(rows_c, w) for w in (down_x, down_d)], axis=1))
    mine_c = jnp.concatenate([matmul_t(rows_c, w) for w in (down_own, down_y)], axis=1)
    grads, contract = elementwise(
        gradient_kernel,
        (mine_b, sent_b, mine_c, sent_c),
        [
            jax.ShapeDtypeStruct((rows_total, 2 * pair), jnp.bfloat16),
            jax.ShapeDtypeStruct((rows_total, 1), jnp.float32),
        ],
    )
    grads_x = with_peer(grads, 2)
    grad_in = (
        matmul_t(grads[:, :pair], gu_own)
        + matmul_t(grads[:, pair:], gu_y)
        + matmul_t(grads_x[:, :pair], gu_x)
        + matmul_t(grads_x[:, pair:], gu_d)
    ).astype(jnp.bfloat16)
    extra = jnp.pad(
        (contract + zeros_b[0, 0] + zeros_c[0, 0]).astype(jnp.bfloat16).reshape(-1, 1, capacity),
        ((0, 0), (0, 3), (0, 128 - capacity)),
    )
    home_b = exchange(jnp.concatenate([grad_in.reshape(-1, block_rows, 128), extra], axis=1))
    home_contract = jnp.sum(
        home_b[:, block_rows, :capacity].astype(jnp.float32).reshape(HALVES, experts, capacity),
        axis=0,
    ).reshape(1, slots_total)
    home_grad = unpack(home_b[:, :block_rows])

    scores_a, share_a, picker_a = route_gates(normed_a, router_cols, ids_a[0])
    mixed_a = sum(
        share_a[:, k : k + 1] * picked(slot_matrix(slots_a, k, slots_total), home_a)
        for k in range(top_count)
    )
    section_a = (values_a + route_scale * mixed_a).astype(jnp.bfloat16)
    next_a = from_behind(section_a[None], "pipe", 1)

    scores_b, share_b, picker_b = route_gates(normed_b, router_cols, ids_b[0])
    picks = [slot_matrix(slots_b, k, slots_total) for k in range(top_count)]
    branch_b = sum(share_b[:, k : k + 1] * picked(picks[k], home_grad) for k in range(top_count))
    contracts = jnp.concatenate(
        [
            jnp.sum(picks[k].astype(jnp.float32) * home_contract, axis=1, keepdims=True)
            for k in range(top_count)
        ],
        axis=1,
    )
    grad_share = route_scale * contracts
    grad_scores = (grad_share - jnp.sum(share_b * grad_share, axis=1, keepdims=True)) / jnp.sum(
        scores_b, axis=1, keepdims=True
    )
    grad_logit = grad_scores * scores_b * (1.0 - scores_b)
    dense_grad = jnp.sum(jnp.where(picker_b, grad_logit[:, :, None], 0.0), axis=1).astype(
        jnp.bfloat16
    )
    router_term = matmul_t(dense_grad, router_cols)
    grad_normed = (route_scale * branch_b + router_term) * gain_row.astype(jnp.float32)
    center = jnp.mean(values_b * grad_normed, axis=-1, keepdims=True)
    grad_values = (
        grad_out.astype(jnp.float32)
        + inverse_b * grad_normed
        - values_b * inverse_b * inverse_b * inverse_b * center
    )
    next_b = from_behind(grad_values.astype(jnp.bfloat16)[None], "pipe", -1)
    return (next_a, next_b)


def solution(mesh):
    return jax.shard_map(
        per_device,
        mesh=mesh,
        in_specs=(
            P("pipe", "expert", None),
            P("pipe", "expert", None),
            P("pipe", "expert", None),
            P("pipe", "expert", None),
            P("pipe", "expert", None),
            P("pipe", None),
            P("pipe", None, None),
            P("pipe", "expert", None, None),
            P("pipe", "expert", None, None),
            P("pipe", "expert", None, None),
        ),
        out_specs=(P("pipe", "expert", None), P("pipe", "expert", None)),
        check_vma=False,
    )
```
